512 devices in a mesh: replica: 32 (over z_hi, x, core), shard: 16 (over z_lo, y).
Axes of the slice: x: 4, y: 8, z: 8 (z_hi: 4, z_lo: 2; z = z_hi * 2 + z_lo), core: 2. Of those that a mesh axis runs over, the one named last changes fastest.
Arguments:
- tokens: bfloat16 [65536, 8192], P(('replica', 'shard')), may hold values from -6 to 6
- cotangent: bfloat16 [65536, 512], P(('replica', 'shard')), may hold values from -0.125 to 0.125
- inner_weight: bfloat16 [32, 8192, 512], P('replica', 'shard'), may hold values from -0.0625 to 0.0625
- fragments: bfloat16 [32, 2, 8192, 512], P('replica', None, 'shard'), may hold values from -12 to 12
- outer_params: float32 [2, 8192, 512], P(None, ('shard', 'replica')), may hold values from -3 to 3
- momentum: float32 [2, 8192, 512], P(None, ('shard', 'replica')), may hold values from -3 to 3
- step_index: int32 [1], replicated, may hold values from 0 to 63
Outputs:
- weight_grad: bfloat16 [32, 8192, 512], P('replica', 'shard')
- new_outer: float32 [2, 8192, 512], P(None, ('shard', 'replica'))
- new_momentum: float32 [2, 8192, 512], P(None, ('shard', 'replica'))
- new_fragment: bfloat16 [32, 8192, 512], P('replica', 'shard')
The draws below stay inside these ranges and needn't reach their ends.
All inputs are finite; a program needn't handle non-finite values.
Results may differ from the reference program's by a relative error of at most 0.012.
Values may be sent and summed in bfloat16 or wider, within the bound.
No kernel may reach another device: no remote copies, remote signals or barrier semaphores. Data moves between devices by JAX's collectives and lax.ppermute only.
A program may use at most 64 MiB of HBM per device.

```python
import jax
import jax.numpy as jnp
from jax import lax

D = 8192
KVW = 512
NFRAG = 2
REPLICAS = 32
TOK_REP = 2048
TOKENS = 65536


def strengthened(drawn, rng, source, target, blocks, factor):
    owner, partner = [(jnp.arange(drawn.shape[dim]) // (drawn.shape[dim] // blocks)).reshape([-1 if axis == dim else 1 for axis in range(drawn.ndim)]) for dim in (source, target)]
    chosen = jax.random.permutation(rng, blocks)[partner]
    strong = (owner == chosen) | (owner == (partner + blocks // 2) % blocks)
    return jnp.where(strong, factor * drawn, drawn)


def block_scale(own_key, dims, pieces, least, high):
    factor_of, own = 1.0, jax.random.fold_in(own_key, 6)
    for position, parts in pieces:
        draws = jnp.exp(jax.random.uniform(jax.random.fold_in(own, position), (parts,), jnp.float32, least / len(pieces), high / len(pieces)))
        factor_of = factor_of * jnp.repeat(draws, dims[position] // parts).reshape([-1 if axis == position else 1 for axis in range(len(dims))])
    return factor_of


def gaussian(rng, shape, width, reach, pieces=(), held_as=jnp.bfloat16):
    result = width * jax.random.normal(rng, shape, jnp.float32)
    if pieces:
        result = result * block_scale(rng, shape, pieces, -0.22, 0.18)
    return jnp.clip(result, -reach, reach).astype(held_as)


def bell_draw_with(key, shape, spread, most, pieces, heavy, dtype=jnp.bfloat16):
    result = spread * jax.random.normal(key, shape, jnp.float32)
    if pieces:
        result = result * block_scale(key, shape, pieces, -0.22, 0.18)
    return jnp.clip(strengthened(result, jax.random.fold_in(key, 3), *heavy), -most, most).astype(dtype)


def setup_inputs(seed: int = 0) -> dict:
    key_of = jax.random.split(jax.random.key(seed), 8)
    tokens = gaussian(key_of[0], (TOKENS, D), 1.0, 6.0, ((0, 512),))
    cotangent = gaussian(key_of[1], (TOKENS, KVW), 0.02, 0.125, ((0, 512),))
    inner_weight = gaussian(key_of[2], (REPLICAS, D, KVW), D ** -0.5, 0.0625, ((0, 32), (1, 16)))
    fragments = bell_draw_with(key_of[3], (REPLICAS, NFRAG, D, KVW), 1.0, 12.0, ((0, 32), (2, 16)), (0, 2, 32, 2.75))
    outer_params = gaussian(key_of[4], (NFRAG, D, KVW), 0.5, 3.0, ((1, 512),), jnp.float32)
    momentum = gaussian(key_of[5], (NFRAG, D, KVW), 0.5, 3.0, ((1, 512),), jnp.float32)
    step_index = jax.random.randint(key_of[6], (1,), 0, 64).astype(jnp.int32)
    return {"tokens": tokens, "cotangent": cotangent, "inner_weight": inner_weight, "fragments": fragments, "outer_params": outer_params, "momentum": momentum, "step_index": step_index}


base_rate = 0.7
decay_rate = 0.9
mix_weight = 0.5

def inner_pass(operands):
    inputs, grads, weight = operands
    projected = jnp.dot(inputs, weight, preferred_element_type=jnp.float32)
    sigmoid_y = jax.nn.sigmoid(projected)
    out_grad = (grads.astype(jnp.float32) * sigmoid_y * (1.0 + projected * (1.0 - sigmoid_y))).astype(jnp.bfloat16)
    summed = lax.dot_general(inputs, out_grad, (((0,), (0,)), ((), ())), preferred_element_type=jnp.float32)
    return summed.astype(jnp.bfloat16)

def reference(tokens, cotangent, inner_weight, fragments, outer_params, momentum, step_index):
    outer_round = step_index[0]
    due_index = (outer_round % NFRAG).astype(jnp.int32)
    outer_rate = base_rate / jnp.sqrt(1.0 + (outer_round // NFRAG).astype(jnp.float32))
    token_blocks = tokens.reshape(REPLICAS, TOK_REP, D)
    grad_blocks = cotangent.reshape(REPLICAS, TOK_REP, KVW)
    weight_grad = lax.map(inner_pass, (token_blocks, grad_blocks, inner_weight))
    local_due = lax.dynamic_index_in_dim(fragments, due_index, 1, keepdims=False)
    mean_local = lax.optimization_barrier(jnp.sum(local_due.astype(jnp.float32), axis=0)) / REPLICAS
    outer_due = lax.dynamic_index_in_dim(outer_params, due_index, 0, keepdims=False)
    moment_due = lax.dynamic_index_in_dim(momentum, due_index, 0, keepdims=False)
    pseudo_grad = outer_due - mean_local
    moment_next = decay_rate * moment_due + pseudo_grad
    outer_next = outer_due - outer_rate * (pseudo_grad + decay_rate * moment_next)
    new_momentum = lax.dynamic_update_index_in_dim(momentum, moment_next, due_index, 0)
    new_outer = lax.dynamic_update_index_in_dim(outer_params, outer_next, due_index, 0)
    outer_half = lax.optimization_barrier(outer_next.astype(jnp.bfloat16))
    new_fragment = (mix_weight * local_due.astype(jnp.float32) + (1.0 - mix_weight) * outer_half.astype(jnp.float32)[None]).astype(jnp.bfloat16)
    return (weight_grad, new_outer, new_momentum, new_fragment)
```

```python
import jax
import jax.numpy as jnp
from jax import lax
from jax.sharding import Mesh
from jax.sharding import PartitionSpec as P

NFRAG = 2
base_rate = 0.7
decay_rate = 0.9
mix_weight = 0.5
REP = ("zh", "x", "c")
SHARD = ("z", "y")
SWAP = [(0, 1), (1, 0)]


def body(tokens, cotangent, inner_weight, fragments, outer_params, momentum, step_index):
    f32, bf16 = jnp.float32, jnp.bfloat16
    z = lax.axis_index("z")
    rows, width = tokens.shape
    ny = lax.axis_size("y")
    feat, cols = inner_weight.shape[1:]
    w = inner_weight[0]

    outer_round = step_index[0]
    due = outer_round % NFRAG
    rate = base_rate / jnp.sqrt(1.0 + (outer_round // NFRAG).astype(f32))

    blocks = tokens.reshape(rows, 2, ny, feat).transpose(2, 0, 1, 3).reshape(ny, rows, 2 * feat)
    x = lax.all_to_all(blocks, "y", split_axis=0, concat_axis=0, tiled=True)
    x = x.reshape(ny * rows, 2 * feat)
    w_other = lax.ppermute(w, "z", SWAP)
    low = jnp.where(z == 0, w, w_other)
    high = jnp.where(z == 0, w_other, w)
    partial = jnp.dot(x, jnp.concatenate([low, high], 0), preferred_element_type=f32)
    partial = partial.astype(bf16).reshape(ny, rows, cols)
    parts = lax.all_to_all(partial, "y", split_axis=0, concat_axis=0, tiled=True)
    y = jnp.sum(parts.astype(f32), 0)
    s = jax.nn.sigmoid(y)
    grad = (cotangent.astype(f32) * s * (1.0 + y * (1.0 - s))).astype(bf16)
    copies = jnp.broadcast_to(grad[None], (ny, rows, cols))
    grads = lax.all_to_all(copies, "y", split_axis=0, concat_axis=0, tiled=True)
    grads = grads.reshape(ny * rows, cols)
    dims = (((0,), (0,)), ((), ()))
    theirs = lax.dynamic_slice_in_dim(x, (1 - z) * feat, feat, 1)
    mine = lax.dynamic_slice_in_dim(x, z * feat, feat, 1)
    away = lax.dot_general(theirs, grads, dims, preferred_element_type=f32).astype(bf16)
    home = lax.dot_general(mine, grads, dims, preferred_element_type=f32)
    weight_grad = (home + lax.ppermute(away, "z", SWAP).astype(f32)).astype(bf16)[None]

    nrep = lax.axis_size(REP)
    own = feat // nrep
    local = lax.dynamic_index_in_dim(fragments[0], due, 0, keepdims=False)
    terms = lax.all_to_all(local.reshape(nrep, own, cols), REP, split_axis=0, concat_axis=0, tiled=True)
    mean_local = jnp.sum(terms.astype(f32), 0) / nrep
    outer_due = lax.dynamic_index_in_dim(outer_params, due, 0, keepdims=False)
    moment_due = lax.dynamic_index_in_dim(momentum, due, 0, keepdims=False)
    pseudo = outer_due - mean_local
    moment_next = decay_rate * moment_due + pseudo
    outer_next = outer_due - rate * (pseudo + decay_rate * moment_next)
    new_momentum = lax.dynamic_update_index_in_dim(momentum, moment_next, due, 0)
    new_outer = lax.dynamic_update_index_in_dim(outer_params, outer_next, due, 0)
    halves = jnp.broadcast_to(outer_next.astype(bf16)[None], (nrep, own, cols))
    half = lax.all_to_all(halves, REP, split_axis=0, concat_axis=0, tiled=True).reshape(feat, cols)
    new_fragment = (mix_weight * local.astype(f32) + (1.0 - mix_weight) * half.astype(f32)).astype(bf16)
    return (weight_grad, new_outer, new_momentum, new_fragment[None])


def solution(mesh):
    fine = Mesh(mesh.devices.reshape(4, 4, 2, 2, 8), REP + SHARD)
    both = REP + SHARD
    placed = (
        P(both, None),
        P(both, None),
        P(REP, SHARD, None),
        P(REP, None, SHARD, None),
        P(None, SHARD + REP, None),
        P(None, SHARD + REP, None),
        P(),
    )
    return jax.shard_map(
        body,
        mesh=fine,
        in_specs=placed,
        out_specs=(P(REP, SHARD, None), P(None, SHARD + REP, None), P(None, SHARD + REP, None), P(REP, SHARD, None)),
        check_vma=False,
    )
```

```python
import functools

import jax
import jax.numpy as jnp
from jax import lax
from jax.experimental import pallas as pl
from jax.experimental.pallas import tpu as pltpu
from jax.sharding import Mesh
from jax.sharding import PartitionSpec as P

NFRAG = 2
base_rate = 0.7
decay_rate = 0.9
mix_weight = 0.5
REP = ("zh1", "zh0", "x1", "x0", "c")
SHARD = ("z", "y")
SWAP = [(0, 1), (1, 0)]
f32, bf16 = jnp.float32, jnp.bfloat16
VMEM = pl.BlockSpec(memory_space=pltpu.VMEM)
PARAMS = pltpu.CompilerParams(vmem_limit_bytes=24 * 2**20)


def pack(tokens, z, ny, feat):
    rows = tokens.shape[0]

    def kernel(z_ref, t_ref, o_ref):
        for j in range(ny):
            o_ref[j] = t_ref[:, j * feat : (j + 1) * feat]

    return pl.pallas_call(
        kernel,
        out_shape=jax.ShapeDtypeStruct((ny, rows, 2 * feat), tokens.dtype),
        grid_spec=pltpu.PrefetchScalarGridSpec(
            num_scalar_prefetch=1,
            grid=(2,),
            in_specs=[pl.BlockSpec((rows, ny * feat), lambda h, z: (0, (h + 1 + z[0]) % 2))],
            out_specs=pl.BlockSpec((ny, rows, feat), lambda h, z: (0, 0, h)),
        ),
        compiler_params=PARAMS,
    )(z[None], tokens)


def project(x, w_other, w, after):
    ny, rows, feat2 = x.shape
    feat, cols = w.shape

    def kernel(x_ref, wo_ref, w_ref, _, o_ref):
        for j in range(ny):
            acc = jnp.dot(x_ref[j, :, :feat], wo_ref[...], preferred_element_type=f32)
            acc += jnp.dot(x_ref[j, :, feat:], w_ref[...], preferred_element_type=f32)
            o_ref[j] = acc.astype(bf16)

    return pl.pallas_call(
        kernel,
        out_shape=jax.ShapeDtypeStruct((ny, rows, cols), bf16),
        in_specs=[VMEM] * 3 + [pl.BlockSpec(memory_space=pl.ANY)],
        out_specs=VMEM,
        compiler_params=PARAMS,
    )(x, w_other, w, after)


def flip(x):
    toks, feats = x.shape
    step = 256

    return pl.pallas_call(
        lambda x_ref, o_ref: o_ref.__setitem__(..., x_ref[...].T),
        out_shape=jax.ShapeDtypeStruct((feats, toks), x.dtype),
        grid=(feats // step,),
        in_specs=[pl.BlockSpec((toks, step), lambda i: (0, i))],
        out_specs=pl.BlockSpec((step, toks), lambda i: (i, 0)),
        compiler_params=PARAMS,
    )(x)


def gate(parts, cotangent, after):
    ny, rows, cols = parts.shape

    def kernel(p_ref, c_ref, _, o_ref):
        y = p_ref[0].astype(f32)
        for j in range(1, ny):
            y += p_ref[j].astype(f32)
        s = jax.nn.sigmoid(y)
        g = (c_ref[...].astype(f32) * s * (1.0 + y * (1.0 - s))).astype(bf16)
        for j in range(ny):
            o_ref[j] = g

    return pl.pallas_call(
        kernel,
        out_shape=jax.ShapeDtypeStruct((ny, rows, cols), bf16),
        in_specs=[VMEM] * 2 + [pl.BlockSpec(memory_space=pl.ANY)],
        out_specs=VMEM,
        compiler_params=PARAMS,
    )(parts, cotangent, after)


def product(xt, grads, first, count, dtype):
    toks, cols = grads.shape
    step = 256

    def kernel(x_ref, g_ref, o_ref):
        for j in range(count // step):
            at = slice(j * step, (j + 1) * step)
            o_ref[at] = jnp.dot(x_ref[at], g_ref[...], preferred_element_type=f32).astype(dtype)

    return pl.pallas_call(
        kernel,
        out_shape=jax.ShapeDtypeStruct((count, cols), dtype),
        grid=(1,),
        in_specs=[
            pl.BlockSpec((count, toks), lambda i: (first // count, 0)),
            pl.BlockSpec((toks, cols), lambda i: (0, 0)),
        ],
        out_specs=pl.BlockSpec((count, cols), lambda i: (0, 0)),
        compiler_params=PARAMS,
    )(xt, grads)


def pick(array, index, axis):
    return lax.dynamic_index_in_dim(array, index, axis, keepdims=False)


def scatter_sum(local):
    total = local
    for axis in reversed(range(len(REP))):
        me = lax.axis_index(REP[axis])
        away = lax.ppermute(pick(total, 1 - me, axis).astype(bf16), REP[axis], SWAP)
        total = pick(total, me, axis).astype(f32) + away.astype(f32)
    return total


def gather(array, axis):
    first = lax.axis_index(REP[axis]) == 0
    other = lax.ppermute(array, REP[axis], SWAP)
    return jnp.stack([jnp.where(first, array, other), jnp.where(first, other, array)], axis)


def update(total, outer, moment, due, rate, count):
    own, cols = total.shape

    def kernel(due_ref, rate_ref, t_ref, o_ref, m_ref, no_ref, nm_ref, half_ref):
        at = due_ref[0]
        no_ref[...] = o_ref[...]
        nm_ref[...] = m_ref[...]
        pseudo = o_ref[at] - t_ref[...] / count
        moment_next = decay_rate * m_ref[at] + pseudo
        outer_next = o_ref[at] - rate_ref[0] * (pseudo + decay_rate * moment_next)
        no_ref[at] = outer_next
        nm_ref[at] = moment_next
        half_ref[...] = outer_next.astype(bf16)

    smem = pl.BlockSpec(memory_space=pltpu.SMEM)
    whole = jax.ShapeDtypeStruct(outer.shape, f32)
    return pl.pallas_call(
        kernel,
        out_shape=[whole, whole, jax.ShapeDtypeStruct((own, cols), bf16)],
        in_specs=[smem, smem, VMEM, VMEM, VMEM],
        out_specs=[VMEM] * 3,
        compiler_params=PARAMS,
    )(due[None], rate[None], total, outer, moment)


def body(tokens, cotangent, inner_weight, fragments, outer_params, momentum, step_index):
    z = lax.axis_index("z")
    rows, width = tokens.shape
    ny = lax.axis_size("y")
    feat, cols = inner_weight.shape[1:]
    w = inner_weight[0]

    outer_round = step_index[0]
    due = outer_round % NFRAG
    rate = base_rate / jnp.sqrt(1.0 + (outer_round // NFRAG).astype(f32))

    nrep = 2 ** len(REP)
    own = feat // nrep
    local = pick(fragments[0], due, 0)
    total = scatter_sum(local.reshape((2,) * len(REP) + (own, cols)))
    new_outer, new_momentum, merged = update(total, outer_params, momentum, due, rate, nrep)

    swap_y = functools.partial(lax.all_to_all, axis_name="y", split_axis=0, concat_axis=0, tiled=True)
    x = swap_y(pack(tokens, z, ny, feat))
    w_other = lax.ppermute(w, "z", SWAP)
    parts = swap_y(project(x, w_other, w, merged))
    xt = flip(x.reshape(ny * rows, 2 * feat))

    for axis in range(len(REP) - 2):
        merged = gather(merged, axis)
    grads = swap_y(gate(parts, cotangent, merged)).reshape(ny * rows, cols)
    for axis in range(len(REP) - 2, len(REP)):
        merged = gather(merged, axis)
    merged = merged.reshape(feat, cols)
    new_fragment = (mix_weight * local.astype(f32) + (1.0 - mix_weight) * merged.astype(f32)).astype(bf16)
    half = feat // 2
    away = [lax.ppermute(product(xt, grads, i * half, half, bf16), "z", SWAP) for i in range(2)]
    home = product(xt, grads, feat, feat, f32)
    weight_grad = (home + jnp.concatenate(away, 0).astype(f32)).astype(bf16)[None]
    return (weight_grad, new_outer, new_momentum, new_fragment[None])


def solution(mesh):
    fine = Mesh(mesh.devices.reshape((2,) * len(REP) + (2, 8)), REP + SHARD)
    both = REP + SHARD
    placed = (
        P(both, None),
        P(both, None),
        P(REP, SHARD, None),
        P(REP, None, SHARD, None),
        P(None, SHARD + REP, None),
        P(None, SHARD + REP, None),
        P(),
    )
    return jax.shard_map(
        body,
        mesh=fine,
        in_specs=placed,
        out_specs=(P(REP, SHARD, None), P(None, SHARD + REP, None), P(None, SHARD + REP, None), P(REP, SHARD, None)),
        check_vma=False,
    )
```

```python
import jax
import jax.numpy as jnp
from jax import lax
from jax.experimental import pallas as pl
from jax.experimental.pallas import tpu as pltpu
from jax.sharding import Mesh
from jax.sharding import PartitionSpec as P

NFRAG = 2
base_rate = 0.7
decay_rate = 0.9
mix_weight = 0.5
REP = ("zh", "x", "c")
SHARD = ("z", "y")
CHIPS = ("c", "z", "y")
SWAP = [(0, 1), (1, 0)]
NZ, NY = 2, 8
LINE, SHIFT = 4, 2
GROUP = NZ * LINE
f32, bf16 = jnp.float32, jnp.bfloat16
VMEM = pl.BlockSpec(memory_space=pltpu.VMEM)
HBM = pl.BlockSpec(memory_space=pltpu.HBM)
ANY = pl.BlockSpec(memory_space=pl.ANY)
PARAMS = pltpu.CompilerParams(vmem_limit_bytes=8 * 2**20)
BIG = pltpu.CompilerParams(vmem_limit_bytes=60 * 2**20)


def place(core, y):
    turned = (y - SHIFT * core) % NY
    return turned // LINE, turned % LINE


def rank(core, z, turned):
    return (core * NZ + z) * NY + (turned + SHIFT * core) % NY


LINES = [
    [rank(core, z, half * LINE + p) for z in range(NZ) for p in range(LINE)]
    for core in range(2)
    for half in range(NY // LINE)
]
MIRROR = [
    (rank(core, z, t), rank(core, z, NY - 1 - t)) for core in range(2) for z in range(NZ) for t in range(NY)
]


def swap_line(array):
    return lax.all_to_all(
        array, CHIPS, split_axis=0, concat_axis=0, axis_index_groups=LINES, tiled=True
    )


def mirror(array):
    return lax.ppermute(array, CHIPS, MIRROR)


def pack(tokens, core, y, feat):
    rows = tokens.shape[0]

    def kernel(core_ref, y_ref, t_ref, o_ref, held, in_sems, out_sems):
        half, _ = place(core_ref[0], y_ref[0])
        loads, stores = [], []
        for j in range(GROUP):
            turned = half * LINE + j % LINE
            for k, at in enumerate((NY - 1 - turned, turned)):
                block = (j // LINE) * NY + (at + SHIFT * core_ref[0]) % NY
                cols = pl.ds(pl.multiple_of(block * feat, feat), feat)
                loads.append(
                    pltpu.make_async_copy(
                        t_ref.at[:, cols], held.at[j, :, pl.ds(k * feat, feat)], in_sems.at[j, k]
                    )
                )
            stores.append(pltpu.make_async_copy(held.at[j], o_ref.at[j], out_sems.at[j]))
        for load in loads:
            load.start()
        for j in range(GROUP):
            loads[2 * j].wait()
            loads[2 * j + 1].wait()
            stores[j].start()
        for store in stores:
            store.wait()

    smem = pl.BlockSpec(memory_space=pltpu.SMEM)
    shape = (GROUP, rows, 2 * feat)
    return pl.pallas_call(
        kernel,
        out_shape=jax.ShapeDtypeStruct(shape, tokens.dtype),
        in_specs=[smem, smem, ANY],
        out_specs=ANY,
        scratch_shapes=[
            pltpu.VMEM(shape, tokens.dtype),
            pltpu.SemaphoreType.DMA((GROUP, 2)),
            pltpu.SemaphoreType.DMA((GROUP,)),
        ],
        compiler_params=BIG,
    )(core[None], y[None], tokens)


def project(x, w_other, w, after):
    n, rows, feat2 = x.shape
    feat, cols = w.shape

    def kernel(x_ref, wo_ref, w_ref, _, o_ref, buf, sems):
        copies = []
        for j in range(n):
            acc = jnp.dot(x_ref[j, :, :feat], wo_ref[...], preferred_element_type=f32)
            acc += jnp.dot(x_ref[j, :, feat:], w_ref[...], preferred_element_type=f32)
            buf[j] = acc.astype(bf16)
            copies.append(pltpu.make_async_copy(buf.at[j], o_ref.at[j], sems.at[j]))
            copies[j].start()
        for copy in copies:
            copy.wait()

    return pl.pallas_call(
        kernel,
        out_shape=jax.ShapeDtypeStruct((n, rows, cols), bf16),
        in_specs=[VMEM] * 3 + [ANY],
        out_specs=HBM,
        scratch_shapes=[pltpu.VMEM((n, rows, cols), bf16), pltpu.SemaphoreType.DMA((n,))],
        compiler_params=PARAMS,
    )(x, w_other, w, after)


def flip(x):
    toks, feats = x.shape
    step = 256

    return pl.pallas_call(
        lambda x_ref, o_ref: o_ref.__setitem__(..., x_ref[...].T),
        out_shape=jax.ShapeDtypeStruct((feats, toks), x.dtype),
        grid=(feats // step,),
        in_specs=[pl.BlockSpec((toks, step), lambda i: (0, i))],
        out_specs=pl.BlockSpec((step, toks), lambda i: (i, 0)),
        compiler_params=PARAMS,
    )(x)


def gate(parts, cotangent, after):
    n, rows, cols = parts.shape

    def kernel(p_ref, c_ref, _, o_ref, buf, sems):
        y = p_ref[0].astype(f32)
        for j in range(1, n):
            y += p_ref[j].astype(f32)
        s = jax.nn.sigmoid(y)
        buf[...] = (c_ref[...].astype(f32) * s * (1.0 + y * (1.0 - s))).astype(bf16)
        copies = [pltpu.make_async_copy(buf, o_ref.at[j], sems.at[j]) for j in range(n)]
        for copy in copies:
            copy.start()
        for copy in copies:
            copy.wait()

    return pl.pallas_call(
        kernel,
        out_shape=jax.ShapeDtypeStruct((n, rows, cols), bf16),
        in_specs=[VMEM] * 2 + [ANY],
        out_specs=HBM,
        scratch_shapes=[pltpu.VMEM((rows, cols), bf16), pltpu.SemaphoreType.DMA((n,))],
        compiler_params=PARAMS,
    )(parts, cotangent, after)


def product(xt, grads, first, count, dtype):
    toks, cols = grads.shape
    step = 256

    def kernel(x_ref, g_ref, o_ref):
        for j in range(count // step):
            at = slice(j * step, (j + 1) * step)
            o_ref[at] = jnp.dot(x_ref[at], g_ref[...], preferred_element_type=f32).astype(dtype)

    return pl.pallas_call(
        kernel,
        out_shape=jax.ShapeDtypeStruct((count, cols), dtype),
        grid=(1,),
        in_specs=[
            pl.BlockSpec((count, toks), lambda i: (first // count, 0)),
            pl.BlockSpec((toks, cols), lambda i: (0, 0)),
        ],
        out_specs=pl.BlockSpec((count, cols), lambda i: (0, 0)),
        compiler_params=PARAMS,
    )(xt, grads)


def call(kernel, out, ins, scalars=()):
    specs = [pl.BlockSpec(memory_space=pltpu.SMEM)] * len(scalars)
    specs += [ANY if isinstance(array, tuple) else VMEM for array in ins]
    return pl.pallas_call(
        kernel,
        out_shape=[jax.ShapeDtypeStruct(shape, dtype) for shape, dtype in out],
        in_specs=specs,
        out_specs=[VMEM] * len(out),
        compiler_params=PARAMS,
    )(*[s[None] for s in scalars], *[array[0] if isinstance(array, tuple) else array for array in ins])


def shifts(arrays, name):
    n = len(arrays) + 1
    return [
        lax.ppermute(array, name, [(i, (i + k) % n) for i in range(n)]) for k, array in enumerate(arrays, 1)
    ]


def first_terms(fragments, due, core):
    nz, nx, nc, own, cols = fragments.shape[1:]

    def kernel(due_ref, core_ref, f_ref, o_ref):
        for i in range(nz):
            for j in range(nx):
                o_ref[i, j] = f_ref[due_ref[0], i, j, 1 - core_ref[0]]

    return call(kernel, [((nz, nx, own, cols), bf16)], [fragments], [due, core])[0]


def x_terms(fragments, away, due, core, x):
    nz, nx, nc, own, cols = fragments.shape[1:]

    def kernel(due_ref, core_ref, x_ref, f_ref, a_ref, *outs):
        for k in range(nx):
            at = (x_ref[0] + k) % nx
            for i in range(nz):
                term = f_ref[due_ref[0], i, at, core_ref[0]].astype(f32) + a_ref[i, at].astype(f32)
                outs[k][i] = term.astype(outs[k].dtype)

    out = [((nz, own, cols), f32)] + [((nz, own, cols), bf16)] * (nx - 1)
    return call(kernel, out, [fragments, away], [due, core, x])


def z_terms(mine, away, z):
    nz, own, cols = mine.shape

    def kernel(z_ref, m_ref, *refs):
        ins, outs = refs[: len(away)], refs[len(away) :]
        for k in range(nz):
            at = (z_ref[0] + k) % nz
            term = m_ref[at]
            for ref in ins:
                term += ref[at].astype(f32)
            outs[k][...] = term.astype(outs[k].dtype)

    out = [((own, cols), f32)] + [((own, cols), bf16)] * (nz - 1)
    return call(kernel, out, [mine, *away], [z])


def update(mine, away, outer, moment, due, rate, count):
    own, cols = mine.shape

    def kernel(due_ref, rate_ref, t_ref, *refs):
        ins = refs[: len(away)]
        o_ref, m_ref, no_ref, nm_ref, half_ref = refs[len(away) :]
        at = due_ref[0]
        no_ref[...] = o_ref[...]
        nm_ref[...] = m_ref[...]
        total = t_ref[...]
        for ref in ins:
            total += ref[...].astype(f32)
        pseudo = o_ref[at] - total / count
        moment_next = decay_rate * m_ref[at] + pseudo
        outer_next = o_ref[at] - rate_ref[0] * (pseudo + decay_rate * moment_next)
        no_ref[at] = outer_next
        nm_ref[at] = moment_next
        half_ref[...] = outer_next.astype(bf16)

    out = [(outer.shape, f32), (outer.shape, f32), ((own, cols), bf16)]
    return call(kernel, out, [mine, *away, outer, moment], [due, rate])


def z_rows(mine, away, z):
    own, cols = mine.shape
    n = len(away) + 1

    def kernel(z_ref, *refs):
        for k in range(n):
            refs[n][(z_ref[0] + n - k) % n] = refs[k][...]

    return call(kernel, [((n, own, cols), bf16)], [mine, *away], [z])[0]


def x_rows(mine, away, x):
    nz, own, cols = mine.shape
    n = len(away) + 1

    def kernel(x_ref, *refs):
        for k in range(n):
            at = (x_ref[0] + n - k) % n
            for i in range(nz):
                refs[n][i, at] = refs[k][i]

    return call(kernel, [((nz, n, own, cols), bf16)], [mine, *away], [x])[0]


def merge(fragments, mine, away, due, core):
    nz, nx, nc, own, cols = fragments.shape[1:]

    def kernel(due_ref, core_ref, f_ref, m_ref, a_ref, o_ref):
        for i in range(nz):
            for j in range(nx):
                for ref, c in ((m_ref, core_ref[0]), (a_ref, 1 - core_ref[0])):
                    local = f_ref[due_ref[0], i, j, c].astype(f32)
                    mixed = mix_weight * local + (1.0 - mix_weight) * ref[i, j].astype(f32)
                    o_ref[i, j, c] = mixed.astype(bf16)

    return call(kernel, [((nz, nx, nc, own, cols), bf16)], [fragments, mine, away], [due, core])[0]


def body(tokens, cotangent, inner_weight, fragments, outer_params, momentum, step_index):
    rows = tokens.shape[0]
    feat, cols = inner_weight.shape[1:]
    w = inner_weight[0]
    zh, xx, core = (lax.axis_index(name) for name in REP)

    outer_round = step_index[0]
    due = outer_round % NFRAG
    rate = base_rate / jnp.sqrt(1.0 + (outer_round // NFRAG).astype(f32))

    x = swap_line(pack(tokens, core, lax.axis_index("y"), feat))
    w_other = mirror(w)

    sizes = tuple(lax.axis_size(name) for name in REP)
    nrep = sizes[0] * sizes[1] * sizes[2]
    local = fragments.reshape((NFRAG, *sizes, feat // nrep, cols))
    away = lax.ppermute(first_terms(local, due, core), "c", SWAP)
    mine, *sent = x_terms(local, away, due, core, xx)
    mine, *sent = z_terms(mine, shifts(sent, "x"), zh)
    new_outer, new_momentum, half = update(mine, shifts(sent, "zh"), outer_params, momentum, due, rate, nrep)

    parts = swap_line(project(x, w_other, w, half))
    line = z_rows(half, shifts([half] * 3, "zh"), zh)
    grads = swap_line(gate(parts, cotangent, line)).reshape(GROUP * rows, cols)
    plane = x_rows(line, shifts([line] * 3, "x"), xx)
    xt = flip(x.reshape(GROUP * rows, 2 * feat))
    piece = feat // 2
    away = [mirror(product(xt, grads, i * piece, piece, bf16)) for i in range(2)]
    new_fragment = merge(local, plane, lax.ppermute(plane, "c", SWAP), due, core)
    home = product(xt, grads, feat, feat, f32)
    weight_grad = (home + jnp.concatenate(away, 0).astype(f32)).astype(bf16)[None]
    return (weight_grad, new_outer, new_momentum, new_fragment.reshape(1, feat, cols))


def solution(mesh):
    fine = Mesh(mesh.devices.reshape(4, 4, 2, NZ, NY), REP + SHARD)
    both = REP + SHARD
    placed = (
        P(both, None),
        P(both, None),
        P(REP, SHARD, None),
        P(REP, None, SHARD, None),
        P(None, SHARD + REP, None),
        P(None, SHARD + REP, None),
        P(),
    )
    return jax.shard_map(
        body,
        mesh=fine,
        in_specs=placed,
        out_specs=(P(REP, SHARD, None), P(None, SHARD + REP, None), P(None, SHARD + REP, None), P(REP, SHARD, None)),
        check_vma=False,
    )
```

```python
import jax
import jax.numpy as jnp
from jax import lax
from jax.experimental import pallas as pl
from jax.experimental.pallas import tpu as pltpu
from jax.sharding import Mesh
from jax.sharding import PartitionSpec as P

NFRAG = 2
base_rate = 0.7
decay_rate = 0.9
mix_weight = 0.5
REP = ("zh", "x", "c")
SHARD = ("z", "y")
CHIPS = ("c", "z", "y")
SWAP = [(0, 1), (1, 0)]
NZ, NY = 2, 8
LINE, SHIFT = 4, 2
GROUP = NZ * LINE
f32, bf16 = jnp.float32, jnp.bfloat16
VMEM = pl.BlockSpec(memory_space=pltpu.VMEM)
HBM = pl.BlockSpec(memory_space=pltpu.HBM)
ANY = pl.BlockSpec(memory_space=pl.ANY)
PARAMS = pltpu.CompilerParams(vmem_limit_bytes=8 * 2**20)
BIG = pltpu.CompilerParams(vmem_limit_bytes=60 * 2**20)


def place(core, y):
    turned = (y - SHIFT * core) % NY
    return turned // LINE, turned % LINE


def rank(core, z, turned):
    return (core * NZ + z) * NY + (turned + SHIFT * core) % NY


LINES = [
    [rank(core, z, half * LINE + p) for z in range(NZ) for p in range(LINE)]
    for core in range(2)
    for half in range(NY // LINE)
]
MIRROR = [
    (rank(core, z, t), rank(core, z, NY - 1 - t)) for core in range(2) for z in range(NZ) for t in range(NY)
]


def swap_line(array):
    return lax.all_to_all(
        array, CHIPS, split_axis=0, concat_axis=0, axis_index_groups=LINES, tiled=True
    )


def mirror(array):
    return lax.ppermute(array, CHIPS, MIRROR)


def pack(tokens, core, y, feat):
    rows = tokens.shape[0]

    def kernel(core_ref, y_ref, t_ref, o_ref, held, in_sems, out_sems):
        half, _ = place(core_ref[0], y_ref[0])
        loads, stores = [], []
        for j in range(GROUP):
            turned = half * LINE + j % LINE
            for k, at in enumerate((NY - 1 - turned, turned)):
                block = (j // LINE) * NY + (at + SHIFT * core_ref[0]) % NY
                cols = pl.ds(pl.multiple_of(block * feat, feat), feat)
                loads.append(
                    pltpu.make_async_copy(
                        t_ref.at[:, cols], held.at[j, :, pl.ds(k * feat, feat)], in_sems.at[j, k]
                    )
                )
            stores.append(pltpu.make_async_copy(held.at[j], o_ref.at[j], out_sems.at[j]))
        for load in loads:
            load.start()
        for j in range(GROUP):
            loads[2 * j].wait()
            loads[2 * j + 1].wait()
            stores[j].start()
        for store in stores:
            store.wait()

    smem = pl.BlockSpec(memory_space=pltpu.SMEM)
    shape = (GROUP, rows, 2 * feat)
    return pl.pallas_call(
        kernel,
        out_shape=jax.ShapeDtypeStruct(shape, tokens.dtype),
        in_specs=[smem, smem, ANY],
        out_specs=ANY,
        scratch_shapes=[
            pltpu.VMEM(shape, tokens.dtype),
            pltpu.SemaphoreType.DMA((GROUP, 2)),
            pltpu.SemaphoreType.DMA((GROUP,)),
        ],
        compiler_params=BIG,
    )(core[None], y[None], tokens)


def project(x, w_other, w, after):
    n, rows, feat2 = x.shape
    feat, cols = w.shape

    def kernel(x_ref, wo_ref, w_ref, _, o_ref):
        for j in range(n):
            acc = jnp.dot(x_ref[j, :, :feat], wo_ref[...], preferred_element_type=f32)
            acc += jnp.dot(x_ref[j, :, feat:], w_ref[...], preferred_element_type=f32)
            o_ref[j] = acc.astype(bf16)

    return pl.pallas_call(
        kernel,
        out_shape=jax.ShapeDtypeStruct((n, rows, cols), bf16),
        in_specs=[VMEM] * 3 + [ANY],
        out_specs=VMEM,
        compiler_params=PARAMS,
    )(x, w_other, w, after)


def gate(parts, cotangent, after):
    n, rows, cols = parts.shape

    def kernel(p_ref, c_ref, _, o_ref):
        y = p_ref[0].astype(f32)
        for j in range(1, n):
            y += p_ref[j].astype(f32)
        s = jax.nn.sigmoid(y)
        g = (c_ref[...].astype(f32) * s * (1.0 + y * (1.0 - s))).astype(bf16)
        for j in range(n):
            o_ref[j] = g

    return pl.pallas_call(
        kernel,
        out_shape=jax.ShapeDtypeStruct((n, rows, cols), bf16),
        in_specs=[VMEM] * 2 + [ANY],
        out_specs=VMEM,
        compiler_params=PARAMS,
    )(parts, cotangent, after)


def product(xt, grads, first, count, dtype):
    toks, cols = grads.shape
    step = 256

    def kernel(x_ref, g_ref, o_ref):
        for j in range(count // step):
            at = slice(j * step, (j + 1) * step)
            o_ref[at] = lax.dot_general(x_ref[:, at], g_ref[...], (((0,), (0,)), ((), ())), preferred_element_type=f32).astype(dtype)

    return pl.pallas_call(
        kernel,
        out_shape=jax.ShapeDtypeStruct((count, cols), dtype),
        grid=(1,),
        in_specs=[
            pl.BlockSpec((toks, count), lambda i: (0, first // count)),
            pl.BlockSpec((toks, cols), lambda i: (0, 0)),
        ],
        out_specs=pl.BlockSpec((count, cols), lambda i: (0, 0)),
        compiler_params=PARAMS,
    )(xt, grads)


def call(kernel, out, ins, scalars=()):
    specs = [pl.BlockSpec(memory_space=pltpu.SMEM)] * len(scalars)
    specs += [ANY if isinstance(array, tuple) else VMEM for array in ins]
    return pl.pallas_call(
        kernel,
        out_shape=[jax.ShapeDtypeStruct(shape, dtype) for shape, dtype in out],
        in_specs=specs,
        out_specs=[VMEM] * len(out),
        compiler_params=PARAMS,
    )(*[s[None] for s in scalars], *[array[0] if isinstance(array, tuple) else array for array in ins])


def shifts(arrays, name):
    n = len(arrays) + 1
    return [
        lax.ppermute(array, name, [(i, (i + k) % n) for i in range(n)]) for k, array in enumerate(arrays, 1)
    ]


def first_terms(fragments, due, core):
    nz, nx, nc, own, cols = fragments.shape[1:]

    def kernel(due_ref, core_ref, f_ref, o_ref):
        for i in range(nz):
            for j in range(nx):
                o_ref[i, j] = f_ref[due_ref[0], i, j, 1 - core_ref[0]]

    return call(kernel, [((nz, nx, own, cols), bf16)], [fragments], [due, core])[0]


def x_terms(fragments, away, due, core, x):
    nz, nx, nc, own, cols = fragments.shape[1:]

    def kernel(due_ref, core_ref, x_ref, f_ref, a_ref, *outs):
        for k in range(nx):
            at = (x_ref[0] + k) % nx
            for i in range(nz):
                term = f_ref[due_ref[0], i, at, core_ref[0]].astype(f32) + a_ref[i, at].astype(f32)
                outs[k][i] = term.astype(outs[k].dtype)

    out = [((nz, own, cols), f32)] + [((nz, own, cols), bf16)] * (nx - 1)
    return call(kernel, out, [fragments, away], [due, core, x])


def z_terms(mine, away, z):
    nz, own, cols = mine.shape

    def kernel(z_ref, m_ref, *refs):
        ins, outs = refs[: len(away)], refs[len(away) :]
        for k in range(nz):
            at = (z_ref[0] + k) % nz
            term = m_ref[at]
            for ref in ins:
                term += ref[at].astype(f32)
            outs[k][...] = term.astype(outs[k].dtype)

    out = [((own, cols), f32)] + [((own, cols), bf16)] * (nz - 1)
    return call(kernel, out, [mine, *away], [z])


def update(mine, away, outer, moment, due, rate, count):
    own, cols = mine.shape

    def kernel(due_ref, rate_ref, t_ref, *refs):
        ins = refs[: len(away)]
        o_ref, m_ref, no_ref, nm_ref, half_ref = refs[len(away) :]
        at = due_ref[0]
        no_ref[...] = o_ref[...]
        nm_ref[...] = m_ref[...]
        total = t_ref[...]
        for ref in ins:
            total += ref[...].astype(f32)
        pseudo = o_ref[at] - total / count
        moment_next = decay_rate * m_ref[at] + pseudo
        outer_next = o_ref[at] - rate_ref[0] * (pseudo + decay_rate * moment_next)
        no_ref[at] = outer_next
        nm_ref[at] = moment_next
        half_ref[...] = outer_next.astype(bf16)

    out = [(outer.shape, f32), (outer.shape, f32), ((own, cols), bf16)]
    return call(kernel, out, [mine, *away, outer, moment], [due, rate])


def z_rows(mine, away, z):
    own, cols = mine.shape
    n = len(away) + 1

    def kernel(z_ref, *refs):
        for k in range(n):
            refs[n][(z_ref[0] + n - k) % n] = refs[k][...]

    return call(kernel, [((n, own, cols), bf16)], [mine, *away], [z])[0]


def x_rows(mine, away, x):
    nz, own, cols = mine.shape
    n = len(away) + 1

    def kernel(x_ref, *refs):
        for k in range(n):
            at = (x_ref[0] + n - k) % n
            for i in range(nz):
                refs[n][i, at] = refs[k][i]

    return call(kernel, [((nz, n, own, cols), bf16)], [mine, *away], [x])[0]


def merge(fragments, mine, away, due, core):
    nz, nx, nc, own, cols = fragments.shape[1:]

    def kernel(due_ref, core_ref, f_ref, m_ref, a_ref, o_ref):
        for i in range(nz):
            for j in range(nx):
                for ref, c in ((m_ref, core_ref[0]), (a_ref, 1 - core_ref[0])):
                    local = f_ref[due_ref[0], i, j, c].astype(f32)
                    mixed = mix_weight * local + (1.0 - mix_weight) * ref[i, j].astype(f32)
                    o_ref[i, j, c] = mixed.astype(bf16)

    return call(kernel, [((nz, nx, nc, own, cols), bf16)], [fragments, mine, away], [due, core])[0]


def body(tokens, cotangent, inner_weight, fragments, outer_params, momentum, step_index):
    rows = tokens.shape[0]
    feat, cols = inner_weight.shape[1:]
    w = inner_weight[0]
    zh, xx, core = (lax.axis_index(name) for name in REP)

    outer_round = step_index[0]
    due = outer_round % NFRAG
    rate = base_rate / jnp.sqrt(1.0 + (outer_round // NFRAG).astype(f32))

    x = swap_line(pack(tokens, core, lax.axis_index("y"), feat))
    w_other = mirror(w)

    sizes = tuple(lax.axis_size(name) for name in REP)
    nrep = sizes[0] * sizes[1] * sizes[2]
    local = fragments.reshape((NFRAG, *sizes, feat // nrep, cols))
    away = lax.ppermute(first_terms(local, due, core), "c", SWAP)
    mine, *sent = x_terms(local, away, due, core, xx)
    mine, *sent = z_terms(mine, shifts(sent, "x"), zh)
    new_outer, new_momentum, half = update(mine, shifts(sent, "zh"), outer_params, momentum, due, rate, nrep)

    parts = swap_line(project(x, w_other, w, half))
    line = z_rows(half, shifts([half] * 3, "zh"), zh)
    grads = swap_line(gate(parts, cotangent, line)).reshape(GROUP * rows, cols)
    plane = x_rows(line, shifts([line] * 3, "x"), xx)
    xt = x.reshape(GROUP * rows, 2 * feat)
    piece = feat // 2
    away = [mirror(product(xt, grads, i * piece, piece, bf16)) for i in range(2)]
    new_fragment = merge(local, plane, lax.ppermute(plane, "c", SWAP), due, core)
    home = product(xt, grads, feat, feat, f32)
    weight_grad = (home + jnp.concatenate(away, 0).astype(f32)).astype(bf16)[None]
    return (weight_grad, new_outer, new_momentum, new_fragment.reshape(1, feat, cols))


def solution(mesh):
    fine = Mesh(mesh.devices.reshape(4, 4, 2, NZ, NY), REP + SHARD)
    both = REP + SHARD
    placed = (
        P(both, None),
        P(both, None),
        P(REP, SHARD, None),
        P(REP, None, SHARD, None),
        P(None, SHARD + REP, None),
        P(None, SHARD + REP, None),
        P(),
    )
    return jax.shard_map(
        body,
        mesh=fine,
        in_specs=placed,
        out_specs=(P(REP, SHARD, None), P(None, SHARD + REP, None), P(None, SHARD + REP, None), P(REP, SHARD, None)),
        check_vma=False,
    )
```

```python
import jax
import jax.numpy as jnp
from jax import lax
from jax.experimental import pallas as pl
from jax.experimental.pallas import tpu as pltpu
from jax.sharding import Mesh
from jax.sharding import PartitionSpec as P

NFRAG = 2
base_rate = 0.7
decay_rate = 0.9
mix_weight = 0.5
REP = ("zh", "x", "c")
SHARD = ("z", "y")
CHIPS = ("c", "z", "y")
SWAP = [(0, 1), (1, 0)]
NZ, NY = 2, 8
LINE, SHIFT = 4, 2
GROUP = NZ * LINE
f32, bf16 = jnp.float32, jnp.bfloat16
VMEM = pl.BlockSpec(memory_space=pltpu.VMEM)
HBM = pl.BlockSpec(memory_space=pltpu.HBM)
ANY = pl.BlockSpec(memory_space=pl.ANY)
PARAMS = pltpu.CompilerParams(vmem_limit_bytes=8 * 2**20)
BIG = pltpu.CompilerParams(vmem_limit_bytes=60 * 2**20)


def place(core, y):
    turned = (y - SHIFT * core) % NY
    return turned // LINE, turned % LINE


def rank(core, z, turned):
    return (core * NZ + z) * NY + (turned + SHIFT * core) % NY


LINES = [
    [rank(core, z, half * LINE + p) for p in range(LINE) for z in range(NZ)]
    for core in range(2)
    for half in range(NY // LINE)
]
MIRROR = [
    (rank(core, z, t), rank(core, z, NY - 1 - t)) for core in range(2) for z in range(NZ) for t in range(NY)
]


def swap_line(array):
    return lax.all_to_all(
        array, CHIPS, split_axis=0, concat_axis=0, axis_index_groups=LINES, tiled=True
    )


def mirror(array):
    return lax.ppermute(array, CHIPS, MIRROR)


def pack(tokens, core, y, feat):
    rows = tokens.shape[0]

    def kernel(core_ref, y_ref, t_ref, o_ref, held, in_sems, out_sems):
        half, _ = place(core_ref[0], y_ref[0])
        loads, stores = [], []
        for j in range(GROUP):
            turned = half * LINE + j // NZ
            for k, at in enumerate((NY - 1 - turned, turned)):
                block = (j % NZ) * NY + (at + SHIFT * core_ref[0]) % NY
                cols = pl.ds(pl.multiple_of(block * feat, feat), feat)
                loads.append(
                    pltpu.make_async_copy(
                        t_ref.at[:, cols], held.at[j, :, pl.ds(k * feat, feat)], in_sems.at[j, k]
                    )
                )
            stores.append(pltpu.make_async_copy(held.at[j], o_ref.at[j], out_sems.at[j]))
        for load in loads:
            load.start()
        for j in range(GROUP):
            loads[2 * j].wait()
            loads[2 * j + 1].wait()
            stores[j].start()
        for store in stores:
            store.wait()

    smem = pl.BlockSpec(memory_space=pltpu.SMEM)
    shape = (GROUP, rows, 2 * feat)
    return pl.pallas_call(
        kernel,
        out_shape=jax.ShapeDtypeStruct(shape, tokens.dtype),
        in_specs=[smem, smem, ANY],
        out_specs=ANY,
        scratch_shapes=[
            pltpu.VMEM(shape, tokens.dtype),
            pltpu.SemaphoreType.DMA((GROUP, 2)),
            pltpu.SemaphoreType.DMA((GROUP,)),
        ],
        compiler_params=BIG,
    )(core[None], y[None], tokens)


def project(x, w_other, w, *after):
    n, rows, feat2 = x.shape
    feat, cols = w.shape
    step = 256

    def kernel(x_ref, wo_ref, w_ref, *refs):
        o_ref, both = refs[len(after) :]
        both[:feat] = wo_ref[...]
        both[feat:] = w_ref[...]
        for i in range(n * rows // step):
            at = slice(i * step, (i + 1) * step)
            o_ref[at] = jnp.dot(x_ref[at], both[...], preferred_element_type=f32).astype(bf16)

    out = pl.pallas_call(
        kernel,
        out_shape=jax.ShapeDtypeStruct((n * rows, cols), bf16),
        in_specs=[VMEM] * 3 + [ANY] * len(after),
        out_specs=VMEM,
        scratch_shapes=[pltpu.VMEM((feat2, cols), bf16)],
        compiler_params=PARAMS,
    )(x.reshape(n * rows, feat2), w_other, w, *after)
    return out.reshape(n, rows, cols)


def gate(parts, cotangent, after):
    n, rows, cols = parts.shape

    def kernel(p_ref, c_ref, _, o_ref):
        y = p_ref[0].astype(f32)
        for j in range(1, n):
            y += p_ref[j].astype(f32)
        s = jax.nn.sigmoid(y)
        g = (c_ref[...].astype(f32) * s * (1.0 + y * (1.0 - s))).astype(bf16)
        for j in range(n):
            o_ref[j] = g

    return pl.pallas_call(
        kernel,
        out_shape=jax.ShapeDtypeStruct((n, rows, cols), bf16),
        in_specs=[VMEM] * 2 + [ANY],
        out_specs=VMEM,
        compiler_params=PARAMS,
    )(parts, cotangent, after)


def product(xt, grads, first, count, dtype):
    toks, cols = grads.shape
    step = 256

    def kernel(x_ref, g_ref, o_ref):
        for j in range(count // step):
            at = slice(j * step, (j + 1) * step)
            o_ref[at] = lax.dot_general(x_ref[:, at], g_ref[...], (((0,), (0,)), ((), ())), preferred_element_type=f32).astype(dtype)

    return pl.pallas_call(
        kernel,
        out_shape=jax.ShapeDtypeStruct((count, cols), dtype),
        grid=(1,),
        in_specs=[
            pl.BlockSpec((toks, count), lambda i: (0, first // count)),
            pl.BlockSpec((toks, cols), lambda i: (0, 0)),
        ],
        out_specs=pl.BlockSpec((count, cols), lambda i: (0, 0)),
        compiler_params=PARAMS,
    )(xt, grads)


def call(kernel, out, ins, scalars=()):
    specs = [pl.BlockSpec(memory_space=pltpu.SMEM)] * len(scalars)
    specs += [ANY if isinstance(array, tuple) else VMEM for array in ins]
    return pl.pallas_call(
        kernel,
        out_shape=[jax.ShapeDtypeStruct(shape, dtype) for shape, dtype in out],
        in_specs=specs,
        out_specs=[VMEM] * len(out),
        compiler_params=PARAMS,
    )(*[s[None] for s in scalars], *[array[0] if isinstance(array, tuple) else array for array in ins])


def shifts(arrays, name):
    n = len(arrays) + 1
    return [
        lax.ppermute(array, name, [(i, (i + k) % n) for i in range(n)]) for k, array in enumerate(arrays, 1)
    ]


def first_terms(fragments, due, core):
    nz, nx, nc, own, cols = fragments.shape[1:]

    def kernel(due_ref, core_ref, f_ref, o_ref):
        for i in range(nz):
            for j in range(nx):
                o_ref[i, j] = f_ref[due_ref[0], i, j, 1 - core_ref[0]]

    return call(kernel, [((nz, nx, own, cols), bf16)], [fragments], [due, core])[0]


def x_terms(fragments, away, due, core, x):
    nz, nx, nc, own, cols = fragments.shape[1:]

    def kernel(due_ref, core_ref, x_ref, f_ref, a_ref, *outs):
        for k in range(nx):
            at = (x_ref[0] + k) % nx
            for i in range(nz):
                term = f_ref[due_ref[0], i, at, core_ref[0]].astype(f32) + a_ref[i, at].astype(f32)
                outs[k][i] = term.astype(outs[k].dtype)

    out = [((nz, own, cols), f32)] + [((nz, own, cols), bf16)] * (nx - 1)
    return call(kernel, out, [fragments, away], [due, core, x])


def z_terms(mine, away, z, w):
    nz, own, cols = mine.shape

    def kernel(z_ref, m_ref, *refs):
        ins, outs = refs[: len(away)], refs[len(away) + 1 :]
        outs[nz][...] = refs[len(away)][...]
        for k in range(nz):
            at = (z_ref[0] + k) % nz
            term = m_ref[at]
            for ref in ins:
                term += ref[at].astype(f32)
            outs[k][...] = term.astype(outs[k].dtype)

    out = [((own, cols), f32)] + [((own, cols), bf16)] * (nz - 1) + [(w.shape, bf16)]
    return call(kernel, out, [mine, *away, w], [z])


def update(mine, away, outer, moment, due, rate, count):
    own, cols = mine.shape

    def kernel(due_ref, rate_ref, t_ref, *refs):
        ins = refs[: len(away)]
        o_ref, m_ref, no_ref, nm_ref, half_ref = refs[len(away) :]
        at = due_ref[0]
        no_ref[...] = o_ref[...]
        nm_ref[...] = m_ref[...]
        total = t_ref[...]
        for ref in ins:
            total += ref[...].astype(f32)
        pseudo = o_ref[at] - total / count
        moment_next = decay_rate * m_ref[at] + pseudo
        outer_next = o_ref[at] - rate_ref[0] * (pseudo + decay_rate * moment_next)
        no_ref[at] = outer_next
        nm_ref[at] = moment_next
        half_ref[...] = outer_next.astype(bf16)

    out = [(outer.shape, f32), (outer.shape, f32), ((own, cols), bf16)]
    return call(kernel, out, [mine, *away, outer, moment], [due, rate])


def z_rows(mine, away, z):
    own, cols = mine.shape
    n = len(away) + 1

    def kernel(z_ref, *refs):
        for k in range(n):
            refs[n][(z_ref[0] + n - k) % n] = refs[k][...]

    return call(kernel, [((n, own, cols), bf16)], [mine, *away], [z])[0]


def x_rows(mine, away, x):
    nz, own, cols = mine.shape
    n = len(away) + 1

    def kernel(x_ref, *refs):
        for k in range(n):
            at = (x_ref[0] + n - k) % n
            for i in range(nz):
                refs[n][i, at] = refs[k][i]

    return call(kernel, [((nz, n, own, cols), bf16)], [mine, *away], [x])[0]


def merge(fragments, mine, away, due, core):
    nz, nx, nc, own, cols = fragments.shape[1:]

    def kernel(due_ref, core_ref, f_ref, m_ref, a_ref, o_ref):
        for i in range(nz):
            for j in range(nx):
                for ref, c in ((m_ref, core_ref[0]), (a_ref, 1 - core_ref[0])):
                    local = f_ref[due_ref[0], i, j, c].astype(f32)
                    mixed = mix_weight * local + (1.0 - mix_weight) * ref[i, j].astype(f32)
                    o_ref[i, j, c] = mixed.astype(bf16)

    return call(kernel, [((nz, nx, nc, own, cols), bf16)], [fragments, mine, away], [due, core])[0]


def body(tokens, cotangent, inner_weight, fragments, outer_params, momentum, step_index):
    rows = tokens.shape[0]
    feat, cols = inner_weight.shape[1:]
    w = inner_weight[0]
    zh, xx, core = (lax.axis_index(name) for name in REP)

    outer_round = step_index[0]
    due = outer_round % NFRAG
    rate = base_rate / jnp.sqrt(1.0 + (outer_round // NFRAG).astype(f32))

    x = swap_line(pack(tokens, core, lax.axis_index("y"), feat))
    w_other = mirror(w)

    sizes = tuple(lax.axis_size(name) for name in REP)
    nrep = sizes[0] * sizes[1] * sizes[2]
    local = fragments.reshape((NFRAG, *sizes, feat // nrep, cols))
    away = lax.ppermute(first_terms(local, due, core), "c", SWAP)
    mine, *sent = x_terms(local, away, due, core, xx)
    mine, *sent, w = z_terms(mine, shifts(sent, "x"), zh, w)
    got = shifts(sent, "zh")
    parts = swap_line(project(x, w_other, w, *got))
    new_outer, new_momentum, half = update(mine, got, outer_params, momentum, due, rate, nrep)

    line = z_rows(half, shifts([half] * 3, "zh"), zh)
    grads = swap_line(gate(parts, cotangent, line)).reshape(GROUP * rows, cols)
    plane = x_rows(line, shifts([line] * 3, "x"), xx)
    xt = x.reshape(GROUP * rows, 2 * feat)
    piece = feat // 2
    away = [mirror(product(xt, grads, i * piece, piece, bf16)) for i in range(2)]
    new_fragment = merge(local, plane, lax.ppermute(plane, "c", SWAP), due, core)
    home = product(xt, grads, feat, feat, f32)
    weight_grad = (home + jnp.concatenate(away, 0).astype(f32)).astype(bf16)[None]
    return (weight_grad, new_outer, new_momentum, new_fragment.reshape(1, feat, cols))


def solution(mesh):
    fine = Mesh(mesh.devices.reshape(4, 4, 2, NZ, NY), REP + SHARD)
    both = REP + SHARD
    placed = (
        P(both, None),
        P(both, None),
        P(REP, SHARD, None),
        P(REP, None, SHARD, None),
        P(None, SHARD + REP, None),
        P(None, SHARD + REP, None),
        P(),
    )
    return jax.shard_map(
        body,
        mesh=fine,
        in_specs=placed,
        out_specs=(P(REP, SHARD, None), P(None, SHARD + REP, None), P(None, SHARD + REP, None), P(REP, SHARD, None)),
        check_vma=False,
    )
```

```python
import jax
import jax.numpy as jnp
from jax import lax
from jax.experimental import pallas as pl
from jax.experimental.pallas import tpu as pltpu
from jax.sharding import Mesh
from jax.sharding import PartitionSpec as P

NFRAG = 2
base_rate = 0.7
decay_rate = 0.9
mix_weight = 0.5
REP = ("zh", "x", "c")
SHARD = ("z", "y")
CHIPS = ("c", "z", "y")
SWAP = [(0, 1), (1, 0)]
NZ, NY = 2, 8
LINE, SHIFT = 4, 2
GROUP = NZ * LINE
f32, bf16 = jnp.float32, jnp.bfloat16
VMEM = pl.BlockSpec(memory_space=pltpu.VMEM)
HBM = pl.BlockSpec(memory_space=pltpu.HBM)
ANY = pl.BlockSpec(memory_space=pl.ANY)
PARAMS = pltpu.CompilerParams(vmem_limit_bytes=8 * 2**20)
BIG = pltpu.CompilerParams(vmem_limit_bytes=60 * 2**20)


def place(core, y):
    turned = (y - SHIFT * core) % NY
    return turned // LINE, turned % LINE


def rank(core, z, turned):
    return (core * NZ + z) * NY + (turned + SHIFT * core) % NY


LINES = [
    [rank(core, z, half * LINE + p) for z in range(NZ) for p in range(LINE)]
    for core in range(2)
    for half in range(NY // LINE)
]
MIRROR = [
    (rank(core, z, t), rank(core, z, NY - 1 - t)) for core in range(2) for z in range(NZ) for t in range(NY)
]


def swap_line(array):
    return lax.all_to_all(
        array, CHIPS, split_axis=0, concat_axis=0, axis_index_groups=LINES, tiled=True
    )


def mirror(array):
    return lax.ppermute(array, CHIPS, MIRROR)


def pack(tokens, core, y, feat):
    rows = tokens.shape[0]

    def kernel(core_ref, y_ref, t_ref, o_ref, held, in_sems, out_sems):
        half, _ = place(core_ref[0], y_ref[0])
        loads, stores = [], []
        for j in range(GROUP):
            turned = half * LINE + j % LINE
            for k, at in enumerate((NY - 1 - turned, turned)):
                block = (j // LINE) * NY + (at + SHIFT * core_ref[0]) % NY
                cols = pl.ds(pl.multiple_of(block * feat, feat), feat)
                loads.append(
                    pltpu.make_async_copy(
                        t_ref.at[:, cols], held.at[j, :, pl.ds(k * feat, feat)], in_sems.at[j, k]
                    )
                )
            stores.append(pltpu.make_async_copy(held.at[j], o_ref.at[j], out_sems.at[j]))
        for load in loads:
            load.start()
        for j in range(GROUP):
            loads[2 * j].wait()
            loads[2 * j + 1].wait()
            stores[j].start()
        for store in stores:
            store.wait()

    smem = pl.BlockSpec(memory_space=pltpu.SMEM)
    shape = (GROUP, rows, 2 * feat)
    return pl.pallas_call(
        kernel,
        out_shape=jax.ShapeDtypeStruct(shape, tokens.dtype),
        in_specs=[smem, smem, ANY],
        out_specs=ANY,
        scratch_shapes=[
            pltpu.VMEM(shape, tokens.dtype),
            pltpu.SemaphoreType.DMA((GROUP, 2)),
            pltpu.SemaphoreType.DMA((GROUP,)),
        ],
        compiler_params=BIG,
    )(core[None], y[None], tokens)


def project(x, w_other, w, after):
    n, rows, feat2 = x.shape
    feat, cols = w.shape
    step = 256

    def kernel(x_ref, wo_ref, w_ref, _, o_ref, both):
        both[:feat] = wo_ref[...]
        both[feat:] = w_ref[...]
        for i in range(n * rows // step):
            at = slice(i * step, (i + 1) * step)
            o_ref[at] = jnp.dot(x_ref[at], both[...], preferred_element_type=f32).astype(bf16)

    out = pl.pallas_call(
        kernel,
        out_shape=jax.ShapeDtypeStruct((n * rows, cols), bf16),
        in_specs=[VMEM] * 3 + [ANY],
        out_specs=VMEM,
        scratch_shapes=[pltpu.VMEM((feat2, cols), bf16)],
        compiler_params=PARAMS,
    )(x.reshape(n * rows, feat2), w_other, w, after)
    return out.reshape(n, rows, cols)


def gate(parts, cotangent, after):
    n, rows, cols = parts.shape

    def kernel(p_ref, c_ref, _, o_ref):
        y = p_ref[0].astype(f32)
        for j in range(1, n):
            y += p_ref[j].astype(f32)
        s = jax.nn.sigmoid(y)
        g = (c_ref[...].astype(f32) * s * (1.0 + y * (1.0 - s))).astype(bf16)
        for j in range(n):
            o_ref[j] = g

    return pl.pallas_call(
        kernel,
        out_shape=jax.ShapeDtypeStruct((n, rows, cols), bf16),
        in_specs=[VMEM] * 2 + [ANY],
        out_specs=VMEM,
        compiler_params=PARAMS,
    )(parts, cotangent, after)


def product(xt, grads, first, count, dtype):
    toks, cols = grads.shape
    step = 256

    def kernel(x_ref, g_ref, o_ref):
        for j in range(count // step):
            at = slice(j * step, (j + 1) * step)
            o_ref[at] = lax.dot_general(x_ref[:, at], g_ref[...], (((0,), (0,)), ((), ())), preferred_element_type=f32).astype(dtype)

    return pl.pallas_call(
        kernel,
        out_shape=jax.ShapeDtypeStruct((count, cols), dtype),
        grid=(1,),
        in_specs=[
            pl.BlockSpec((toks, count), lambda i: (0, first // count)),
            pl.BlockSpec((toks, cols), lambda i: (0, 0)),
        ],
        out_specs=pl.BlockSpec((count, cols), lambda i: (0, 0)),
        compiler_params=PARAMS,
    )(xt, grads)


def call(kernel, out, ins, scalars=()):
    specs = [pl.BlockSpec(memory_space=pltpu.SMEM)] * len(scalars)
    specs += [ANY if isinstance(array, tuple) else VMEM for array in ins]
    return pl.pallas_call(
        kernel,
        out_shape=[jax.ShapeDtypeStruct(shape, dtype) for shape, dtype in out],
        in_specs=specs,
        out_specs=[VMEM] * len(out),
        compiler_params=PARAMS,
    )(*[s[None] for s in scalars], *[array[0] if isinstance(array, tuple) else array for array in ins])


def shifts(arrays, name):
    n = len(arrays) + 1
    return [
        lax.ppermute(array, name, [(i, (i + k) % n) for i in range(n)]) for k, array in enumerate(arrays, 1)
    ]


def first_terms(fragments, due, core):
    nz, nx, nc, own, cols = fragments.shape[1:]

    def kernel(due_ref, core_ref, f_ref, o_ref):
        for i in range(nz):
            for j in range(nx):
                o_ref[i, j] = f_ref[due_ref[0], i, j, 1 - core_ref[0]]

    return call(kernel, [((nz, nx, own, cols), bf16)], [fragments], [due, core])[0]


def x_terms(fragments, away, due, core, x, *ahead):
    nz, nx, nc, own, cols = fragments.shape[1:]

    def kernel(due_ref, core_ref, x_ref, f_ref, a_ref, *refs):
        outs = refs[len(ahead) :]
        for k in range(nx):
            at = (x_ref[0] + k) % nx
            for i in range(nz):
                term = f_ref[due_ref[0], i, at, core_ref[0]].astype(f32) + a_ref[i, at].astype(f32)
                outs[k][i] = term.astype(outs[k].dtype)

    out = [((nz, own, cols), f32)] + [((nz, own, cols), bf16)] * (nx - 1)
    return call(kernel, out, [fragments, away, *ahead], [due, core, x])


def z_terms(mine, away, z, w):
    nz, own, cols = mine.shape

    def kernel(z_ref, m_ref, *refs):
        ins, outs = refs[: len(away)], refs[len(away) + 1 :]
        outs[nz][...] = refs[len(away)][...]
        for k in range(nz):
            at = (z_ref[0] + k) % nz
            term = m_ref[at]
            for ref in ins:
                term += ref[at].astype(f32)
            outs[k][...] = term.astype(outs[k].dtype)

    out = [((own, cols), f32)] + [((own, cols), bf16)] * (nz - 1) + [(w.shape, bf16)]
    return call(kernel, out, [mine, *away, w], [z])


def update(mine, away, outer, moment, due, rate, count):
    own, cols = mine.shape

    def kernel(due_ref, rate_ref, t_ref, *refs):
        ins = refs[: len(away)]
        o_ref, m_ref, no_ref, nm_ref, half_ref = refs[len(away) :]
        at = due_ref[0]
        no_ref[...] = o_ref[...]
        nm_ref[...] = m_ref[...]
        total = t_ref[...]
        for ref in ins:
            total += ref[...].astype(f32)
        pseudo = o_ref[at] - total / count
        moment_next = decay_rate * m_ref[at] + pseudo
        outer_next = o_ref[at] - rate_ref[0] * (pseudo + decay_rate * moment_next)
        no_ref[at] = outer_next
        nm_ref[at] = moment_next
        half_ref[...] = outer_next.astype(bf16)

    out = [(outer.shape, f32), (outer.shape, f32), ((own, cols), bf16)]
    return call(kernel, out, [mine, *away, outer, moment], [due, rate])


def z_rows(mine, away, z):
    own, cols = mine.shape
    n = len(away) + 1

    def kernel(z_ref, *refs):
        for k in range(n):
            refs[n][(z_ref[0] + n - k) % n] = refs[k][...]

    return call(kernel, [((n, own, cols), bf16)], [mine, *away], [z])[0]


def x_rows(mine, away, x):
    nz, own, cols = mine.shape
    n = len(away) + 1

    def kernel(x_ref, *refs):
        for k in range(n):
            at = (x_ref[0] + n - k) % n
            for i in range(nz):
                refs[n][i, at] = refs[k][i]

    return call(kernel, [((nz, n, own, cols), bf16)], [mine, *away], [x])[0]


def merge(fragments, mine, away, due, core):
    nz, nx, nc, own, cols = fragments.shape[1:]

    def kernel(due_ref, core_ref, f_ref, m_ref, a_ref, o_ref):
        for i in range(nz):
            for j in range(nx):
                for ref, c in ((m_ref, core_ref[0]), (a_ref, 1 - core_ref[0])):
                    local = f_ref[due_ref[0], i, j, c].astype(f32)
                    mixed = mix_weight * local + (1.0 - mix_weight) * ref[i, j].astype(f32)
                    o_ref[i, j, c] = mixed.astype(bf16)

    return call(kernel, [((nz, nx, nc, own, cols), bf16)], [fragments, mine, away], [due, core])[0]


def body(tokens, cotangent, inner_weight, fragments, outer_params, momentum, step_index):
    rows = tokens.shape[0]
    feat, cols = inner_weight.shape[1:]
    w = inner_weight[0]
    zh, xx, core = (lax.axis_index(name) for name in REP)

    outer_round = step_index[0]
    due = outer_round % NFRAG
    rate = base_rate / jnp.sqrt(1.0 + (outer_round // NFRAG).astype(f32))

    x = swap_line(pack(tokens, core, lax.axis_index("y"), feat))
    w_other = mirror(w)

    sizes = tuple(lax.axis_size(name) for name in REP)
    nrep = sizes[0] * sizes[1] * sizes[2]
    local = fragments.reshape((NFRAG, *sizes, feat // nrep, cols))
    away = lax.ppermute(first_terms(local, due, core), "c", SWAP)
    mine, *sent = x_terms(local, away, due, core, xx, outer_params, momentum)
    mine, *sent, w = z_terms(mine, shifts(sent, "x"), zh, w)
    new_outer, new_momentum, half = update(mine, shifts(sent, "zh"), outer_params, momentum, due, rate, nrep)

    parts = swap_line(project(x, w_other, w, half))
    line = z_rows(half, shifts([half] * 3, "zh"), zh)
    grads = swap_line(gate(parts, cotangent, line)).reshape(GROUP * rows, cols)
    plane = x_rows(line, shifts([line] * 3, "x"), xx)
    xt = x.reshape(GROUP * rows, 2 * feat)
    piece = feat // 2
    away = [mirror(product(xt, grads, i * piece, piece, bf16)) for i in range(2)]
    new_fragment = merge(local, plane, lax.ppermute(plane, "c", SWAP), due, core)
    home = product(xt, grads, feat, feat, f32)
    weight_grad = (home + jnp.concatenate(away, 0).astype(f32)).astype(bf16)[None]
    return (weight_grad, new_outer, new_momentum, new_fragment.reshape(1, feat, cols))


def solution(mesh):
    fine = Mesh(mesh.devices.reshape(4, 4, 2, NZ, NY), REP + SHARD)
    both = REP + SHARD
    placed = (
        P(both, None),
        P(both, None),
        P(REP, SHARD, None),
        P(REP, None, SHARD, None),
        P(None, SHARD + REP, None),
        P(None, SHARD + REP, None),
        P(),
    )
    return jax.shard_map(
        body,
        mesh=fine,
        in_specs=placed,
        out_specs=(P(REP, SHARD, None), P(None, SHARD + REP, None), P(None, SHARD + REP, None), P(REP, SHARD, None)),
        check_vma=False,
    )
```
